256 devices in a mesh: blk: 128 (over z, x, y_hi, core), tm: 2 (over y_lo).
Axes of the slice: x: 4, y: 4 (y_hi: 2, y_lo: 2; y = y_hi * 2 + y_lo), z: 8, core: 2. Of those that a mesh axis runs over, the one named last changes fastest.
Arguments:
- history: bfloat16 [4, 32768, 512], P(None, 'blk', 'tm'), may hold values from -6 to 6
- panel_pos: bfloat16 [3, 32768], P(None, 'blk'), may hold values from -2 to 2, as said below
- area: bfloat16 [32768], P('blk'), may hold values from 0.5 to 2
- observer_pos: float32 [3, 131072], P(None, 'blk'), may hold values from -2 to 2, as said below
- delays: int32 [128, 7], P('blk'), may hold values from -64 to 64, as said below
Outputs:
- pressure: float32 [131072, 512], P('blk', 'tm')
The draws below stay inside these ranges and needn't reach their ends.
Inputs may be any that keep to these rules, and one draw needn't show every extreme that they name: `delays`: -64 and 64 are both taken. `observer_pos`: the third coordinate (height) of every observer is 0.1 or more. `panel_pos`: the third coordinate (height) of every panel centre is 0 or less.
All inputs are finite; a program needn't handle non-finite values.
Results may differ from the reference program's by a relative error of at most 0.0034.
Values may be sent and summed in bfloat16 or wider, within the bound.
A program may use at most 128 MiB of HBM per device.

```python
import math
import jax
import jax.numpy as jnp
from jax import lax

OBS_DEV = 1024
PB = 256
TIME = 512
MAXLAG = 64
HALF = 3
SPAN = 7
NBLK = 128
OBSERVERS = 131072
PANELS = 32768


def draw_panel_pos(key, part):
    key = jax.random.fold_in(key, 3)
    key_plane, key_depth = jax.random.split(key)
    plane = jax.random.uniform(key_plane, (2, PANELS), jnp.float32, -2.0, 2.0)
    depth = jax.random.uniform(key_depth, (1, PANELS), jnp.float32, -0.2, 0.0)
    return jnp.concatenate([plane, depth], axis=0).astype(jnp.bfloat16)


def draw_observer_pos(key, part):
    key = jax.random.fold_in(key, 5)
    key_plane, key_height = jax.random.split(key)
    plane = jax.random.uniform(key_plane, (2, OBSERVERS), jnp.float32, -2.0, 2.0)
    height = jax.random.uniform(key_height, (1, OBSERVERS), jnp.float32, 0.1, 1.0)
    return jnp.concatenate([plane, height], axis=0).astype(jnp.float32)


def draw_delays(key, part):
    key = jax.random.fold_in(key, 11)
    key_vals, key_row, key_cols = jax.random.split(key, 3)
    values = jax.random.randint(key_vals, (NBLK, SPAN), -MAXLAG, MAXLAG + 1)
    row_low = jax.random.randint(key_row, (), 0, NBLK)
    row_high = (row_low + 1) % NBLK
    columns = jax.random.randint(key_cols, (2,), 0, SPAN)
    values = values.at[row_low, columns[0]].set(-MAXLAG)
    values = values.at[row_high, columns[1]].set(MAXLAG)
    return values.astype(jnp.int32)


def levels(stream_key, extent, pieces, smallest, largest):
    def one(position, parts):
        draws = jax.random.uniform(jax.random.fold_in(jax.random.fold_in(stream_key, 6), position), (parts,), jnp.float32, smallest / len(pieces), largest / len(pieces))
        return jnp.repeat(jnp.exp(draws), extent[position] // parts).reshape((-1,) + (1,) * (len(extent) - position - 1))

    factor_of = one(*pieces[0])
    for cut in pieces[1:]:
        factor_of = factor_of * one(*cut)
    return factor_of


def scatter_about(own_key, shape, spread, reach, cuts=(), kind=jnp.bfloat16):
    level = levels(own_key, shape, cuts, -0.22, 0.18) if cuts else 1.0
    drawn = jax.random.normal(own_key, shape, jnp.float32) * spread * level
    return jnp.minimum(jnp.maximum(drawn, -reach), reach).astype(kind)


def setup_inputs(seed: int = 0) -> dict:
    arg_keys = jax.random.split(jax.random.key(seed), 6)
    history = scatter_about(arg_keys[0], (4, PANELS, TIME), 1.0, 6.0, ((1, 128), (2, 2)))
    panel_pos = draw_panel_pos(jax.random.fold_in(arg_keys[5], 71), 0)
    area = jnp.clip(jnp.exp(math.log(2.0) - 1.3862944 * jax.random.uniform(arg_keys[2], (PANELS,), jnp.float32) ** levels(arg_keys[2], (PANELS,), ((0, 128),), -0.2, 0.2)), 0.5, 2.0).astype(jnp.bfloat16)
    observer_pos = draw_observer_pos(jax.random.fold_in(arg_keys[5], 71), 0)
    delays = draw_delays(jax.random.fold_in(arg_keys[5], 71), 0)
    return dict(history=history, panel_pos=panel_pos, area=area, observer_pos=observer_pos, delays=delays)


four_pi = 4.0 * math.pi

def pair_weights(observers, positions, areas):
    apart = observers[:, :, None] - positions[:, None, :]
    distance = jnp.sqrt(lax.optimization_barrier(jnp.sum(apart * apart, axis=0)))
    inverse = 1.0 / distance
    scaled = areas[None, :] * inverse / four_pi
    loads_fast = scaled[None] * apart * inverse[None]
    loads_slow = loads_fast * inverse[None]
    stacked = jnp.stack([scaled, loads_fast[0], loads_fast[1], loads_fast[2], loads_slow[0], loads_slow[1], loads_slow[2]], axis=1)
    return stacked.reshape(observers.shape[1], 7 * positions.shape[1]).astype(jnp.bfloat16)

def block_signal(source, first_index, sample_count):
    padded = jnp.pad(source, ((0, 0), (0, 0), (MAXLAG + 1, MAXLAG + 1)))
    segment = lax.dynamic_slice_in_dim(padded, (first_index + MAXLAG).astype(jnp.int32), sample_count + 2, 2)
    values = segment[:, :, 1:-1].astype(jnp.float32)
    slopes = 0.5 * (segment[:, :, 2:].astype(jnp.float32) - segment[:, :, :-2].astype(jnp.float32))
    stacked = jnp.concatenate([slopes, values[1:]], axis=0).astype(jnp.bfloat16)
    return stacked.reshape(7 * source.shape[1], sample_count)

def reference(history, panel_pos, area, observer_pos, delays):

    def one_block(observer_block):
        observers = lax.dynamic_slice_in_dim(observer_pos, (observer_block * OBS_DEV).astype(jnp.int32), OBS_DEV, 1)
        total = jnp.zeros((OBS_DEV, TIME), jnp.float32)
        for column in range(SPAN):
            panel_block = (observer_block + column - HALF) % NBLK
            first_panel = (panel_block * PB).astype(jnp.int32)
            positions = lax.dynamic_slice_in_dim(panel_pos, first_panel, PB, 1).astype(jnp.float32)
            areas = lax.dynamic_slice_in_dim(area, first_panel, PB, 0).astype(jnp.float32)
            source = lax.dynamic_slice_in_dim(history, first_panel, PB, 1)
            delay_steps = delays[observer_block, column].astype(jnp.int32)
            weights = pair_weights(observers, positions, areas)
            signals = block_signal(source, -delay_steps, TIME)
            total = total + jnp.dot(weights, signals, preferred_element_type=jnp.float32)
        return total
    blocks = lax.map(one_block, jnp.arange(NBLK, dtype=jnp.int32))
    return blocks.reshape(OBSERVERS, TIME)
```

```python
import functools
import math

import jax
import jax.numpy as jnp
from jax import lax
from jax.experimental import pallas as pl
from jax.experimental.pallas import tpu as pltpu
from jax.sharding import PartitionSpec as P

MESH = pl.DeviceIdType.MESH
MAIN, HALO = 256, 80
EXT = MAIN + HALO
STAGE = HALO + MAIN + HALO
COEF = 7
INV_FOUR_PI = 1.0 / (4.0 * math.pi)
OWN, SIB, ACROSS, SIDE, SIB_ACROSS, RELAY, SIB_RELAY = range(7)
HEAD, GEOM = 4, 5


def kernel(history, place, area, observers, delays, out,
           ext, geom, weights, signals, stage, spread,
           send_sem, recv_sem, halo_send, halo_recv):
    g = lax.axis_index("blk")
    half = lax.axis_index("tm")
    blocks = lax.axis_size("blk")
    core = g % 2
    upper = (g // 2) % 2
    sign = 1 - 2 * upper
    inner = (core + upper) % 2
    sibling = g + 1 - 2 * core
    across = g + 2 * sign
    ahead = (g + 4 * sign + blocks) % blocks
    behind = (g - 4 * sign + blocks) % blocks
    beside = (sibling + 4 * sign * (2 * inner - 1) + blocks) % blocks
    target = {SIB: sibling, ACROSS: across, SIDE: beside, SIB_ACROSS: sibling, RELAY: ahead, SIB_RELAY: sibling}
    origin = {SIB: OWN, ACROSS: OWN, SIDE: OWN, SIB_ACROSS: ACROSS, RELAY: ACROSS, SIB_RELAY: RELAY}
    slot = {OWN: 3, SIB: 4 - 2 * inner, ACROSS: 5, SIDE: 6 * inner, SIB_ACROSS: 6 - 2 * inner, RELAY: 1,
            SIB_RELAY: 2 - 2 * inner}

    barrier = pltpu.get_barrier_semaphore()
    for device in (sibling, across, ahead, behind, beside):
        pl.semaphore_signal(barrier, inc=1, device_id=(device, half), device_id_type=MESH)
    pl.semaphore_signal(barrier, inc=1, device_id=(g, 1 - half), device_id_type=MESH)

    geom[OWN] = jnp.zeros((8, 256), jnp.float32)
    geom[OWN, 0:3, :] = place[...].astype(jnp.float32)
    geom[OWN, 3:4, :] = area[...].astype(jnp.float32) * INV_FOUR_PI

    def flip(c):
        ext[OWN, c, 0:MAIN, :] = history[c].T

    def copy(edge, part):
        source, dest = origin[edge], edge
        if part == GEOM:
            src, dst = geom.at[source], geom.at[dest]
        elif part == HEAD:
            src, dst = ext.at[source, 0, pl.ds(MAIN, HALO)], ext.at[dest, 0, pl.ds(MAIN, HALO)]
        elif part == 0 and source == OWN:
            src, dst = ext.at[source, 0, pl.ds(0, MAIN)], ext.at[dest, 0, pl.ds(0, MAIN)]
        else:
            src, dst = ext.at[source, part], ext.at[dest, part]
        return pltpu.make_async_remote_copy(
            src_ref=src, dst_ref=dst, send_sem=send_sem.at[edge - 1, part], recv_sem=recv_sem.at[edge - 1, part],
            device_id=(target[edge], half), device_id_type=MESH)

    def halo(c):
        first = pl.multiple_of((MAIN - HALO) * (1 - half), 16)
        return pltpu.make_async_remote_copy(
            src_ref=ext.at[OWN, c, pl.ds(first, HALO)], dst_ref=ext.at[OWN, c, pl.ds(MAIN, HALO)],
            send_sem=halo_send.at[c], recv_sem=halo_recv.at[c], device_id=(g, 1 - half), device_id_type=MESH)

    def fill_weights(buf):
        @pl.loop(0, 32)
        def _(i):
            rows = pl.ds(pl.multiple_of(i * 32, 32), 32)
            for lane in (0, 128):
                cols = pl.ds(lane, 128)
                dx = spread[0, rows, :] - geom[buf, 0:1, cols]
                dy = spread[1, rows, :] - geom[buf, 1:2, cols]
                dz = spread[2, rows, :] - geom[buf, 2:3, cols]
                inv = lax.rsqrt(dx * dx + dy * dy + dz * dz)
                s = geom[buf, 3:4, cols] * inv
                fast = s * inv
                slow = fast * inv
                for n, value in enumerate((s, fast * dx, fast * dy, fast * dz, slow * dx, slow * dy, slow * dz)):
                    weights[buf, rows, pl.ds(n * 256 + lane, 128)] = value.astype(jnp.bfloat16)

    def delay_of(buf):
        m = slot[buf]
        return delays[0, m + upper * (6 - 2 * m)]

    def fill_signals(buf, c):
        k = delay_of(buf)
        edge = ext[buf, c, MAIN:EXT, :].astype(jnp.float32)
        zero = jnp.zeros_like(edge)
        late = half == 1
        for lane in (0, 1):
            cols = slice(lane * 128, lane * 128 + 128)
            stage[lane, 0:HALO, :] = jnp.where(late, edge, zero)[:, cols]
            stage[lane, HALO:HALO + MAIN, :] = ext[buf, c, 0:MAIN, cols].astype(jnp.float32)
            stage[lane, HALO + MAIN:STAGE, :] = jnp.where(late, zero, edge)[:, cols]
            after = stage[lane, pl.ds(HALO + 1 - k, MAIN), :]
            before = stage[lane, pl.ds(HALO - 1 - k, MAIN), :]
            at = c * 256 + lane * 128
            signals[:, at:at + 128] = (0.5 * (after - before)).astype(jnp.bfloat16)
            if c:
                signals[:, at + 768:at + 896] = stage[lane, pl.ds(HALO - k, MAIN), :].astype(jnp.bfloat16)

    def multiply(buf, first):
        @pl.loop(0, 2)
        def _(i):
            rows = pl.ds(pl.multiple_of(i * 512, 512), 512)
            part = lax.dot_general(weights[buf, rows, :], signals[...], (((1,), (1,)), ((), ())),
                                   preferred_element_type=jnp.float32)
            if first:
                out[rows, :] = part
            else:
                out[rows, :] += part

    def contribute(buf, first=False):
        for c in range(4):
            fill_signals(buf, c)
        multiply(buf, first)

    mine = (ACROSS, SIDE, SIB)
    flip(0)
    pl.semaphore_wait(barrier, 6)
    for edge in mine:
        copy(edge, GEOM).start()
    halo(0).start()
    for edge in mine:
        copy(edge, 0).start()
    for c in range(1, 4):
        flip(c)
        halo(c).start()
    for axis in range(3):
        for i in range(8):
            line = observers[axis:axis + 1, i * 128:(i + 1) * 128]
            spread[axis, i * 128:(i + 1) * 128, :] = jnp.broadcast_to(line, (128, 128)).T
    halo(0).wait_recv()
    for edge in mine:
        copy(edge, HEAD).start()
    for c in range(1, 4):
        halo(c).wait_recv()
        for edge in mine:
            copy(edge, c).start()

    def arrived(edge, part):
        copy(edge, part).wait_recv()
        if part == 0 and origin[edge] == OWN:
            copy(edge, HEAD).wait_recv()

    def relay(edge, part):
        arrived(edge, part)
        if edge == ACROSS:
            copy(RELAY, part).start()
            copy(SIB_ACROSS, part).start()
        else:
            copy(SIB_RELAY, part).start()

    fill_weights(OWN)
    relay(ACROSS, GEOM)
    copy(SIB, GEOM).wait_recv()
    fill_weights(SIB)
    copy(SIDE, GEOM).wait_recv()
    fill_weights(SIDE)
    fill_weights(ACROSS)
    relay(ACROSS, 0)
    copy(SIB_ACROSS, GEOM).wait_recv()
    fill_weights(SIB_ACROSS)
    contribute(OWN, True)
    relay(ACROSS, 1)
    relay(RELAY, GEOM)
    fill_weights(RELAY)
    copy(SIB_RELAY, GEOM).wait_recv()
    fill_weights(SIB_RELAY)
    relay(ACROSS, 2)
    for c in range(4):
        arrived(SIB, c)
    contribute(SIB)
    relay(RELAY, 0)
    relay(ACROSS, 3)
    for c in range(4):
        arrived(SIDE, c)
    contribute(SIDE)
    relay(RELAY, 1)
    contribute(ACROSS)
    for c in range(4):
        arrived(SIB_ACROSS, c)
    contribute(SIB_ACROSS)
    relay(RELAY, 2)
    relay(RELAY, 3)
    contribute(RELAY)
    for c in range(4):
        arrived(SIB_RELAY, c)
    contribute(SIB_RELAY)

    for c in range(4):
        halo(c).wait_send()
    for edge in target:
        for part in range(6):
            if part != HEAD or origin[edge] == OWN:
                copy(edge, part).wait_send()


def per_device(history, panel_pos, area, observer_pos, delays):
    vmem = pl.BlockSpec(memory_space=pltpu.VMEM)
    return pl.pallas_call(
        kernel,
        out_shape=jax.ShapeDtypeStruct((1024, 256), jnp.float32),
        in_specs=[vmem, vmem, vmem, vmem, pl.BlockSpec(memory_space=pltpu.SMEM)],
        out_specs=vmem,
        scratch_shapes=[
            pltpu.VMEM((7, 4, EXT, 256), jnp.bfloat16),
            pltpu.VMEM((7, 8, 256), jnp.float32),
            pltpu.VMEM((7, 1024, COEF * 256), jnp.bfloat16),
            pltpu.VMEM((256, COEF * 256), jnp.bfloat16),
            pltpu.VMEM((2, STAGE, 128), jnp.float32),
            pltpu.VMEM((3, 1024, 128), jnp.float32),
            pltpu.SemaphoreType.DMA((6, 6)),
            pltpu.SemaphoreType.DMA((6, 6)),
            pltpu.SemaphoreType.DMA((4,)),
            pltpu.SemaphoreType.DMA((4,)),
        ],
        compiler_params=pltpu.CompilerParams(
            collective_id=0, has_side_effects=True, vmem_limit_bytes=56 * 1024 * 1024),
        cost_estimate=pl.CostEstimate(flops=6_580_000_000, bytes_accessed=2_000_000, transcendentals=1_900_000),
    )(history, panel_pos, area.reshape(1, 256), observer_pos, delays)


def solution(mesh):
    return jax.shard_map(
        per_device,
        mesh=mesh,
        in_specs=(P(None, "blk", "tm"), P(None, "blk"), P("blk"), P(None, "blk"), P("blk", None)),
        out_specs=P("blk", "tm"),
        check_vma=False,
    )
```

```python
import math

import jax
import jax.numpy as jnp
from jax import lax
from jax.experimental import pallas as pl
from jax.experimental.pallas import tpu as pltpu
from jax.sharding import PartitionSpec as P

MESH = pl.DeviceIdType.MESH
MAIN, HALO = 256, 80
BODY = MAIN - HALO
EXT = MAIN + HALO
STAGE = HALO + MAIN + HALO
COEF = 7
INV_FOUR_PI = 1.0 / (4.0 * math.pi)
OWN, SIB, ACROSS, SIDE, SIB_ACROSS, RELAY, SIB_RELAY = range(7)
EDGE, OUTER, GEOM = 4, 5, 6


def kernel(history, place, area, observers, delays, out,
           ext, geom, weights, signals, stage, spread, lags, send_sem, recv_sem):
    g = lax.axis_index("blk")
    half = lax.axis_index("tm")
    blocks = lax.axis_size("blk")
    core = g % 2
    upper = (g // 2) % 2
    sign = 1 - 2 * upper
    inner = (core + upper) % 2
    sibling = g + 1 - 2 * core
    across = g + 2 * sign
    ahead = (g + 4 * sign + blocks) % blocks
    behind = (g - 4 * sign + blocks) % blocks
    beside = (sibling + 4 * sign * (2 * inner - 1) + blocks) % blocks
    facing = g + inner * sign
    target = {SIB: sibling, ACROSS: across, SIDE: beside, SIB_ACROSS: sibling, RELAY: ahead, SIB_RELAY: sibling}
    origin = {SIB: OWN, ACROSS: OWN, SIDE: OWN, SIB_ACROSS: ACROSS, RELAY: ACROSS, SIB_RELAY: RELAY}
    slot = {OWN: 3, SIB: 4 - 2 * inner, ACROSS: 5, SIDE: 6 * inner, SIB_ACROSS: 6 - 2 * inner, RELAY: 1,
            SIB_RELAY: 2 - 2 * inner}
    edge_rows = pl.ds(pl.multiple_of(BODY * (1 - half), 16), HALO)
    body_rows = pl.ds(pl.multiple_of(HALO * half, 16), BODY)
    outer_rows = pl.ds(MAIN, HALO)

    barrier = pltpu.get_barrier_semaphore()
    for device, part in ((sibling, half), (across, half), (ahead, half), (behind, half), (beside, half),
                         (g, 1 - half), (across, 1 - half), (facing, 1 - half)):
        pl.semaphore_signal(barrier, inc=1, device_id=(device, part), device_id_type=MESH)

    geom[OWN] = jnp.zeros((8, 256), jnp.float32)
    geom[OWN, 0:3, :] = place[...].astype(jnp.float32)
    geom[OWN, 3:4, :] = area[...].astype(jnp.float32).reshape(1, 256) * INV_FOUR_PI
    for buf, m in slot.items():
        lags[buf] = delays[0, m + upper * (6 - 2 * m)]

    def flip(c):
        ext[OWN, c, 0:MAIN, :] = history[c].T

    def view(buf, part):
        if part == GEOM:
            return geom.at[buf]
        if part == EDGE:
            return ext.at[buf, :, edge_rows]
        if part == OUTER:
            return ext.at[buf, :, outer_rows]
        return ext.at[buf, part, body_rows]

    def copy(buf, part):
        if part == OUTER and buf in (OWN, ACROSS, RELAY):
            source = {OWN: OWN, ACROSS: OWN, RELAY: RELAY - (RELAY - SIDE) * inner}[buf]
            device = {OWN: g, ACROSS: across, RELAY: facing}[buf]
            src, where = view(source, EDGE), (device, 1 - half)
        else:
            src, where = view(origin[buf], part), (target[buf], half)
        return pltpu.make_async_remote_copy(
            src_ref=src, dst_ref=view(buf, part), send_sem=send_sem.at[buf, part], recv_sem=recv_sem.at[buf, part],
            device_id=where, device_id_type=MESH)

    def fill_weights(buf):
        @pl.loop(0, 16, unroll=4)
        def _(i):
            rows = pl.ds(pl.multiple_of(i * 64, 64), 64)
            ox, oy, oz = (spread[n, rows, :] for n in range(3))
            for lane in (0, 128):
                cols = pl.ds(lane, 128)
                dx = ox - geom[buf, 0:1, cols]
                dy = oy - geom[buf, 1:2, cols]
                dz = oz - geom[buf, 2:3, cols]
                inv = lax.rsqrt(dx * dx + dy * dy + dz * dz)
                s = geom[buf, 3:4, cols] * inv
                fast = s * inv
                fx, fy, fz = fast * dx, fast * dy, fast * dz
                for n, value in enumerate((s, fx, fx * inv, fy, fy * inv, fz, fz * inv)):
                    weights[buf, rows, pl.ds(n * 256 + lane, 128)] = value.astype(jnp.bfloat16)

    def fill_signals(buf, c):
        k = lags[buf]
        edge = ext[buf, c, MAIN:EXT, :].astype(jnp.float32)
        zero = jnp.zeros_like(edge)
        late = half == 1
        for lane in (0, 1):
            cols = slice(lane * 128, lane * 128 + 128)
            stage[lane, 0:HALO, :] = jnp.where(late, edge, zero)[:, cols]
            stage[lane, HALO:HALO + MAIN, :] = ext[buf, c, 0:MAIN, cols].astype(jnp.float32)
            stage[lane, HALO + MAIN:STAGE, :] = jnp.where(late, zero, edge)[:, cols]
            after = stage[lane, pl.ds(HALO + 1 - k, MAIN), :]
            before = stage[lane, pl.ds(HALO - 1 - k, MAIN), :]
            at = max(2 * c - 1, 0) * 256 + lane * 128
            signals[at:at + 128, :] = (0.5 * (after - before)).astype(jnp.bfloat16).T
            if c:
                signals[at + 256:at + 384, :] = stage[lane, pl.ds(HALO - k, MAIN), :].astype(jnp.bfloat16).T

    def contribute(buf, channels=(0, 1, 2, 3), first=False):
        for c in channels:
            fill_signals(buf, c)
        cols = slice(max(2 * channels[0] - 1, 0) * 256, (2 * channels[-1] + 1) * 256)
        part = jnp.dot(weights[buf, :, cols], signals[cols, :], preferred_element_type=jnp.float32)
        if first:
            out[...] = part
        else:
            out[...] += part

    def arrived(buf, *parts):
        for part in parts:
            copy(buf, part).wait_recv()

    def send(part, *bufs):
        for buf in bufs:
            copy(buf, part).start()

    def relay(buf, part):
        arrived(buf, part)
        if buf == RELAY:
            send(part, SIB_RELAY)
        elif part == OUTER:
            send(part, SIB_ACROSS)
        else:
            send(part, RELAY, SIB_ACROSS)

    flip(0)
    pl.semaphore_wait(barrier, 8)
    send(GEOM, ACROSS, SIDE, SIB)
    send(0, ACROSS, SIDE, SIB)
    flip(1)
    send(1, ACROSS, SIDE, SIB)
    flip(2)
    flip(3)
    send(EDGE, ACROSS, SIDE)
    send(OUTER, OWN, ACROSS)
    send(2, ACROSS, SIDE)
    send(3, ACROSS, SIDE)
    send(EDGE, SIB)
    send(2, SIB)
    send(3, SIB)
    for axis in range(3):
        for i in range(8):
            line = observers[axis:axis + 1, i * 128:(i + 1) * 128]
            spread[axis, i * 128:(i + 1) * 128, :] = jnp.broadcast_to(line, (128, 128)).T

    fill_weights(OWN)
    relay(ACROSS, GEOM)
    arrived(SIB, GEOM)
    fill_weights(SIB)
    relay(ACROSS, 0)
    arrived(SIDE, GEOM)
    fill_weights(SIDE)
    relay(ACROSS, 1)
    fill_weights(ACROSS)
    arrived(SIB_ACROSS, GEOM)
    fill_weights(SIB_ACROSS)
    relay(ACROSS, EDGE)
    relay(RELAY, GEOM)
    arrived(OWN, OUTER)
    send(OUTER, SIDE, SIB)
    fill_weights(RELAY)
    relay(RELAY, 0)
    relay(ACROSS, OUTER)
    contribute(OWN, first=True)
    relay(ACROSS, 2)
    arrived(SIB_RELAY, GEOM)
    fill_weights(SIB_RELAY)
    relay(RELAY, 1)
    arrived(SIB, 0, 1, EDGE, OUTER, 2, 3)
    contribute(SIB)
    relay(ACROSS, 3)
    relay(RELAY, EDGE)
    arrived(SIDE, 0, 1, EDGE, 2, 3)
    send(OUTER, RELAY)
    arrived(SIDE, OUTER)
    contribute(SIDE)
    relay(RELAY, 2)
    contribute(ACROSS)
    relay(RELAY, OUTER)
    arrived(SIB_ACROSS, 0, 1, EDGE, OUTER, 2, 3)
    contribute(SIB_ACROSS)
    relay(RELAY, 3)
    contribute(RELAY)
    arrived(SIB_RELAY, 0, 1, EDGE, OUTER, 2, 3)
    contribute(SIB_RELAY)

    for buf in range(7):
        for part in range(7):
            if buf != OWN or part == OUTER:
                copy(buf, part).wait_send()


def per_device(history, panel_pos, area, observer_pos, delays):
    vmem = pl.BlockSpec(memory_space=pltpu.VMEM)
    return pl.pallas_call(
        kernel,
        out_shape=jax.ShapeDtypeStruct((1024, 256), jnp.float32),
        in_specs=[vmem, vmem, vmem, vmem, pl.BlockSpec(memory_space=pltpu.SMEM)],
        out_specs=vmem,
        scratch_shapes=[
            pltpu.VMEM((7, 4, EXT, 256), jnp.bfloat16),
            pltpu.VMEM((7, 8, 256), jnp.float32),
            pltpu.VMEM((7, 1024, COEF * 256), jnp.bfloat16),
            pltpu.VMEM((COEF * 256, 256), jnp.bfloat16),
            pltpu.VMEM((2, STAGE, 128), jnp.float32),
            pltpu.VMEM((3, 1024, 128), jnp.float32),
            pltpu.SMEM((8,), jnp.int32),
            pltpu.SemaphoreType.DMA((7, 7)),
            pltpu.SemaphoreType.DMA((7, 7)),
        ],
        compiler_params=pltpu.CompilerParams(
            collective_id=0, has_side_effects=True, vmem_limit_bytes=56 * 1024 * 1024),
        cost_estimate=pl.CostEstimate(flops=6_580_000_000, bytes_accessed=2_000_000, transcendentals=1_900_000),
    )(history, panel_pos, area, observer_pos, delays)


def solution(mesh):
    return jax.shard_map(
        per_device,
        mesh=mesh,
        in_specs=(P(None, "blk", "tm"), P(None, "blk"), P("blk"), P(None, "blk"), P("blk", None)),
        out_specs=P("blk", "tm"),
        check_vma=False,
    )
```

```python
import math

import jax
import jax.numpy as jnp
from jax import lax
from jax.experimental import pallas as pl
from jax.experimental.pallas import tpu as pltpu
from jax.sharding import PartitionSpec as P

MESH = pl.DeviceIdType.MESH
MAIN, HALO = 256, 80
BODY = MAIN - HALO
EXT = MAIN + HALO
STAGE = HALO + MAIN + HALO
COEF = 7
INV_FOUR_PI = 1.0 / (4.0 * math.pi)
OWN, SIB, ACROSS, SIDE, SIB_ACROSS, RELAY, SIB_RELAY = range(7)
EDGE, OUTER, GEOM = 4, 5, 6


def kernel(history, place, area, observers, delays, out,
           ext, geom, weights, signals, stage, spread, lags, send_sem, recv_sem):
    g = lax.axis_index("blk")
    half = lax.axis_index("tm")
    blocks = lax.axis_size("blk")
    core = g % 2
    upper = (g // 2) % 2
    sign = 1 - 2 * upper
    inner = (core + upper) % 2
    sibling = g + 1 - 2 * core
    across = g + 2 * sign
    ahead = (g + 4 * sign + blocks) % blocks
    behind = (g - 4 * sign + blocks) % blocks
    beside = (sibling + 4 * sign * (2 * inner - 1) + blocks) % blocks
    facing = g + inner * sign
    target = {SIB: sibling, ACROSS: across, SIDE: beside, SIB_ACROSS: sibling, RELAY: ahead, SIB_RELAY: sibling}
    origin = {SIB: OWN, ACROSS: OWN, SIDE: OWN, SIB_ACROSS: ACROSS, RELAY: ACROSS, SIB_RELAY: RELAY}
    slot = {OWN: 3, SIB: 4 - 2 * inner, ACROSS: 5, SIDE: 6 * inner, SIB_ACROSS: 6 - 2 * inner, RELAY: 1,
            SIB_RELAY: 2 - 2 * inner}
    edge_rows = pl.ds(pl.multiple_of(BODY * (1 - half), 16), HALO)
    body_rows = pl.ds(pl.multiple_of(HALO * half, 16), BODY)
    outer_rows = pl.ds(MAIN, HALO)

    barrier = pltpu.get_barrier_semaphore()
    for device, part in ((sibling, half), (across, half), (ahead, half), (behind, half), (beside, half),
                         (g, 1 - half), (across, 1 - half), (facing, 1 - half)):
        pl.semaphore_signal(barrier, inc=1, device_id=(device, part), device_id_type=MESH)

    geom[OWN] = jnp.zeros((8, 256), jnp.float32)
    geom[OWN, 0:3, :] = place[...].astype(jnp.float32)
    geom[OWN, 3:4, :] = area[...].astype(jnp.float32).reshape(1, 256) * INV_FOUR_PI
    for buf, m in slot.items():
        lags[buf] = delays[0, m + upper * (6 - 2 * m)]

    def flip(c):
        ext[OWN, c, 0:MAIN, :] = history[c].T

    def view(buf, part):
        if part == GEOM:
            return geom.at[buf]
        if part == EDGE:
            return ext.at[buf, :, edge_rows]
        if part == OUTER:
            return ext.at[buf, :, outer_rows]
        return ext.at[buf, part, body_rows]

    def copy(buf, part):
        if part == OUTER and buf in (OWN, ACROSS, RELAY):
            source = {OWN: OWN, ACROSS: OWN, RELAY: RELAY - (RELAY - SIDE) * inner}[buf]
            device = {OWN: g, ACROSS: across, RELAY: facing}[buf]
            src, where = view(source, EDGE), (device, 1 - half)
        else:
            src, where = view(origin[buf], part), (target[buf], half)
        return pltpu.make_async_remote_copy(
            src_ref=src, dst_ref=view(buf, part), send_sem=send_sem.at[buf, part], recv_sem=recv_sem.at[buf, part],
            device_id=where, device_id_type=MESH)

    def fill_weights(buf):
        @pl.loop(0, 16, unroll=4)
        def _(i):
            rows = pl.ds(pl.multiple_of(i * 64, 64), 64)
            ox, oy, oz = (spread[n, rows, :] for n in range(3))
            for lane in (0, 128):
                cols = pl.ds(lane, 128)
                dx = ox - geom[buf, 0:1, cols]
                dy = oy - geom[buf, 1:2, cols]
                dz = oz - geom[buf, 2:3, cols]
                inv = lax.rsqrt(dx * dx + dy * dy + dz * dz)
                s = geom[buf, 3:4, cols] * inv
                fast = s * inv
                fx, fy, fz = fast * dx, fast * dy, fast * dz
                for n, value in enumerate((s, fx, fx * inv, fy, fy * inv, fz, fz * inv)):
                    weights[buf, rows, pl.ds(n * 256 + lane, 128)] = value.astype(jnp.bfloat16)

    def fill_signals(buf, c):
        k = lags[buf]
        edge = ext[buf, c, MAIN:EXT, :].astype(jnp.float32)
        zero = jnp.zeros_like(edge)
        late = half == 1
        for lane in (0, 1):
            cols = slice(lane * 128, lane * 128 + 128)
            stage[lane, 0:HALO, :] = jnp.where(late, edge, zero)[:, cols]
            stage[lane, HALO:HALO + MAIN, :] = ext[buf, c, 0:MAIN, cols].astype(jnp.float32)
            stage[lane, HALO + MAIN:STAGE, :] = jnp.where(late, zero, edge)[:, cols]
            after = stage[lane, pl.ds(HALO + 1 - k, MAIN), :]
            before = stage[lane, pl.ds(HALO - 1 - k, MAIN), :]
            at = max(2 * c - 1, 0) * 256 + lane * 128
            signals[at:at + 128, :] = (0.5 * (after - before)).astype(jnp.bfloat16).T
            if c:
                signals[at + 256:at + 384, :] = stage[lane, pl.ds(HALO - k, MAIN), :].astype(jnp.bfloat16).T

    def contribute(buf, channels=(0, 1, 2, 3), first=False):
        for c in channels:
            fill_signals(buf, c)
        cols = slice(max(2 * channels[0] - 1, 0) * 256, (2 * channels[-1] + 1) * 256)
        part = jnp.dot(weights[buf, :, cols], signals[cols, :], preferred_element_type=jnp.float32)
        if first:
            out[...] = part
        else:
            out[...] += part

    def arrived(buf, *parts):
        for part in parts:
            copy(buf, part).wait_recv()

    def send(part, *bufs):
        for buf in bufs:
            copy(buf, part).start()

    def relay(buf, part):
        arrived(buf, part)
        if buf == RELAY:
            send(part, SIB_RELAY)
        elif part == OUTER:
            send(part, SIB_ACROSS)
        else:
            send(part, RELAY, SIB_ACROSS)

    flip(0)
    pl.semaphore_wait(barrier, 8)
    send(GEOM, ACROSS, SIDE, SIB)
    send(0, ACROSS, SIDE, SIB)
    flip(1)
    send(1, ACROSS, SIDE, SIB)
    flip(2)
    flip(3)
    send(EDGE, ACROSS, SIDE)
    send(OUTER, OWN, ACROSS)
    send(2, ACROSS, SIDE)
    send(3, ACROSS, SIDE)
    send(EDGE, SIB)
    send(2, SIB)
    send(3, SIB)
    for axis in range(3):
        for i in range(8):
            line = observers[axis:axis + 1, i * 128:(i + 1) * 128]
            spread[axis, i * 128:(i + 1) * 128, :] = jnp.broadcast_to(line, (128, 128)).T

    fill_weights(OWN)
    relay(ACROSS, GEOM)
    arrived(SIB, GEOM)
    fill_weights(SIB)
    relay(ACROSS, 0)
    arrived(SIDE, GEOM)
    fill_weights(SIDE)
    relay(ACROSS, 1)
    fill_weights(ACROSS)
    arrived(SIB_ACROSS, GEOM)
    fill_weights(SIB_ACROSS)
    relay(ACROSS, EDGE)
    relay(RELAY, GEOM)
    arrived(OWN, OUTER)
    send(OUTER, SIDE, SIB)
    fill_weights(RELAY)
    relay(RELAY, 0)
    relay(ACROSS, OUTER)
    relay(ACROSS, 2)
    arrived(SIB_RELAY, GEOM)
    fill_weights(SIB_RELAY)
    relay(RELAY, 1)
    relay(ACROSS, 3)
    out[...] = jnp.zeros_like(out)

    @pl.loop(0, 7)
    def _(buf):
        @pl.when(buf == SIB)
        def _():
            arrived(SIB, 0, 1, EDGE, OUTER, 2, 3)
            relay(RELAY, EDGE)
            arrived(SIDE, 0, 1, EDGE, 2, 3)
            send(OUTER, RELAY)

        @pl.when(buf == SIDE)
        def _():
            arrived(SIDE, OUTER)
            arrived(SIB_ACROSS, 0, 1, EDGE, OUTER, 2, 3)

        @pl.when(buf == ACROSS)
        def _():
            relay(RELAY, 2)

        @pl.when(buf == SIB_ACROSS)
        def _():
            relay(RELAY, OUTER)
            relay(RELAY, 3)

        @pl.when(buf == SIB_RELAY)
        def _():
            arrived(SIB_RELAY, 0, 1, EDGE, OUTER, 2, 3)

        contribute(buf)

    for buf in range(7):
        for part in range(7):
            if buf != OWN or part == OUTER:
                copy(buf, part).wait_send()


def per_device(history, panel_pos, area, observer_pos, delays):
    vmem = pl.BlockSpec(memory_space=pltpu.VMEM)
    return pl.pallas_call(
        kernel,
        out_shape=jax.ShapeDtypeStruct((1024, 256), jnp.float32),
        in_specs=[vmem, vmem, vmem, vmem, pl.BlockSpec(memory_space=pltpu.SMEM)],
        out_specs=vmem,
        scratch_shapes=[
            pltpu.VMEM((7, 4, EXT, 256), jnp.bfloat16),
            pltpu.VMEM((7, 8, 256), jnp.float32),
            pltpu.VMEM((7, 1024, COEF * 256), jnp.bfloat16),
            pltpu.VMEM((COEF * 256, 256), jnp.bfloat16),
            pltpu.VMEM((2, STAGE, 128), jnp.float32),
            pltpu.VMEM((3, 1024, 128), jnp.float32),
            pltpu.SMEM((8,), jnp.int32),
            pltpu.SemaphoreType.DMA((7, 7)),
            pltpu.SemaphoreType.DMA((7, 7)),
        ],
        compiler_params=pltpu.CompilerParams(
            collective_id=0, has_side_effects=True, vmem_limit_bytes=56 * 1024 * 1024),
        cost_estimate=pl.CostEstimate(flops=6_580_000_000, bytes_accessed=2_000_000, transcendentals=1_900_000),
    )(history, panel_pos, area, observer_pos, delays)


def solution(mesh):
    return jax.shard_map(
        per_device,
        mesh=mesh,
        in_specs=(P(None, "blk", "tm"), P(None, "blk"), P("blk"), P(None, "blk"), P("blk", None)),
        out_specs=P("blk", "tm"),
        check_vma=False,
    )
```

```python
import math

import jax
import jax.numpy as jnp
from jax import lax
from jax.experimental import pallas as pl
from jax.experimental.pallas import tpu as pltpu
from jax.sharding import PartitionSpec as P

MESH = pl.DeviceIdType.MESH
MAIN, HALO = 256, 80
BODY = MAIN - HALO
EXT = MAIN + HALO
STAGE = HALO + MAIN + HALO
COEF = 7
INV_FOUR_PI = 1.0 / (4.0 * math.pi)
OWN, SIB, ACROSS, SIDE, SIB_ACROSS, RELAY, SIB_RELAY = range(7)
EDGE, OUTER, GEOM = 4, 5, 6


def kernel(history, place, area, observers, delays, out,
           ext, geom, weights, signals, stage, spread, lags, send_sem, recv_sem):
    g = lax.axis_index("blk")
    half = lax.axis_index("tm")
    blocks = lax.axis_size("blk")
    core = g % 2
    upper = (g // 2) % 2
    sign = 1 - 2 * upper
    inner = (core + upper) % 2
    sibling = g + 1 - 2 * core
    across = g + 2 * sign
    ahead = (g + 4 * sign + blocks) % blocks
    behind = (g - 4 * sign + blocks) % blocks
    beside = (sibling + 4 * sign * (2 * inner - 1) + blocks) % blocks
    facing = g + inner * sign
    target = {SIB: sibling, ACROSS: across, SIDE: beside, SIB_ACROSS: sibling, RELAY: ahead, SIB_RELAY: sibling}
    origin = {SIB: OWN, ACROSS: OWN, SIDE: OWN, SIB_ACROSS: ACROSS, RELAY: ACROSS, SIB_RELAY: RELAY}
    slot = {OWN: 3, SIB: 4 - 2 * inner, ACROSS: 5, SIDE: 6 * inner, SIB_ACROSS: 6 - 2 * inner, RELAY: 1,
            SIB_RELAY: 2 - 2 * inner}
    edge_rows = pl.ds(pl.multiple_of(BODY * (1 - half), 16), HALO)
    body_rows = pl.ds(pl.multiple_of(HALO * half, 16), BODY)
    outer_rows = pl.ds(MAIN, HALO)

    barrier = pltpu.get_barrier_semaphore()
    for device, part in ((sibling, half), (across, half), (ahead, half), (behind, half), (beside, half),
                         (g, 1 - half), (across, 1 - half), (facing, 1 - half)):
        pl.semaphore_signal(barrier, inc=1, device_id=(device, part), device_id_type=MESH)

    geom[OWN] = jnp.zeros((8, 256), jnp.float32)
    geom[OWN, 0:3, :] = place[...].astype(jnp.float32)
    geom[OWN, 3:4, :] = area[...].astype(jnp.float32).reshape(1, 256) * INV_FOUR_PI
    for buf, m in slot.items():
        lags[buf] = delays[0, m + upper * (6 - 2 * m)]

    def flip(c):
        ext[OWN, c, 0:MAIN, :] = history[c].T

    def view(buf, part):
        if part == GEOM:
            return geom.at[buf]
        if part == EDGE:
            return ext.at[buf, :, edge_rows]
        if part == OUTER:
            return ext.at[buf, :, outer_rows]
        return ext.at[buf, part, body_rows]

    def copy(buf, part):
        if part == OUTER and buf in (OWN, ACROSS, RELAY):
            source = {OWN: OWN, ACROSS: OWN, RELAY: RELAY - (RELAY - SIDE) * inner}[buf]
            device = {OWN: g, ACROSS: across, RELAY: facing}[buf]
            src, where = view(source, EDGE), (device, 1 - half)
        else:
            src, where = view(origin[buf], part), (target[buf], half)
        return pltpu.make_async_remote_copy(
            src_ref=src, dst_ref=view(buf, part), send_sem=send_sem.at[buf, part], recv_sem=recv_sem.at[buf, part],
            device_id=where, device_id_type=MESH)

    def fill_weights(buf):
        @pl.loop(0, 16, unroll=4)
        def _(i):
            rows = pl.ds(pl.multiple_of(i * 64, 64), 64)
            ox, oy, oz = (spread[n, rows, :] for n in range(3))
            for lane in (0, 128):
                cols = pl.ds(lane, 128)
                dx = ox - geom[buf, 0:1, cols]
                dy = oy - geom[buf, 1:2, cols]
                dz = oz - geom[buf, 2:3, cols]
                inv = lax.rsqrt(dx * dx + dy * dy + dz * dz)
                s = geom[buf, 3:4, cols] * inv
                fast = s * inv
                fx, fy, fz = fast * dx, fast * dy, fast * dz
                for n, value in enumerate((s, fx, fx * inv, fy, fy * inv, fz, fz * inv)):
                    weights[buf, rows, pl.ds(n * 256 + lane, 128)] = value.astype(jnp.bfloat16)

    def fill_signals(buf, c):
        k = lags[buf]
        edge = ext[buf, c, MAIN:EXT, :].astype(jnp.float32)
        zero = jnp.zeros_like(edge)
        late = half == 1
        for lane in (0, 1):
            cols = slice(lane * 128, lane * 128 + 128)
            stage[lane, 0:HALO, :] = jnp.where(late, edge, zero)[:, cols]
            stage[lane, HALO:HALO + MAIN, :] = ext[buf, c, 0:MAIN, cols].astype(jnp.float32)
            stage[lane, HALO + MAIN:STAGE, :] = jnp.where(late, zero, edge)[:, cols]
            after = stage[lane, pl.ds(HALO + 1 - k, MAIN), :]
            before = stage[lane, pl.ds(HALO - 1 - k, MAIN), :]
            at = max(2 * c - 1, 0) * 256 + lane * 128
            signals[at:at + 128, :] = (0.5 * (after - before)).astype(jnp.bfloat16).T
            if c:
                signals[at + 256:at + 384, :] = stage[lane, pl.ds(HALO - k, MAIN), :].astype(jnp.bfloat16).T

    def contribute(buf, channels=(0, 1, 2, 3), first=False):
        for c in channels:
            fill_signals(buf, c)
        cols = slice(max(2 * channels[0] - 1, 0) * 256, (2 * channels[-1] + 1) * 256)
        part = jnp.dot(weights[buf, :, cols], signals[cols, :], preferred_element_type=jnp.float32)
        if first:
            out[...] = part
        else:
            out[...] += part

    def arrived(buf, *parts):
        for part in parts:
            copy(buf, part).wait_recv()

    def send(part, *bufs):
        for buf in bufs:
            copy(buf, part).start()

    def relay(buf, part):
        arrived(buf, part)
        if buf == RELAY:
            send(part, SIB_RELAY)
        elif part == OUTER:
            send(part, SIB_ACROSS)
        else:
            send(part, RELAY, SIB_ACROSS)

    for axis in range(3):
        for i in range(8):
            line = observers[axis:axis + 1, i * 128:(i + 1) * 128]
            spread[axis, i * 128:(i + 1) * 128, :] = jnp.broadcast_to(line, (128, 128)).T
    flip(0)
    pl.semaphore_wait(barrier, 8)
    send(GEOM, ACROSS, SIDE, SIB)
    send(0, ACROSS, SIDE, SIB)
    flip(1)
    send(1, ACROSS, SIDE, SIB)
    flip(2)
    flip(3)
    send(EDGE, ACROSS, SIDE)
    send(OUTER, OWN, ACROSS)
    send(2, ACROSS, SIDE)
    send(3, ACROSS, SIDE)
    send(EDGE, SIB)
    send(2, SIB)
    send(3, SIB)

    fill_weights(OWN)
    relay(ACROSS, GEOM)
    arrived(SIB, GEOM)
    fill_weights(SIB)
    relay(ACROSS, 0)
    arrived(SIDE, GEOM)
    fill_weights(SIDE)
    relay(ACROSS, 1)
    fill_weights(ACROSS)
    arrived(SIB_ACROSS, GEOM)
    fill_weights(SIB_ACROSS)
    relay(ACROSS, EDGE)
    relay(RELAY, GEOM)
    arrived(OWN, OUTER)
    send(OUTER, SIDE, SIB)
    fill_weights(RELAY)
    relay(RELAY, 0)
    relay(ACROSS, OUTER)
    relay(ACROSS, 2)
    arrived(SIB_RELAY, GEOM)
    fill_weights(SIB_RELAY)
    relay(RELAY, 1)
    relay(ACROSS, 3)
    out[...] = jnp.zeros_like(out)

    @pl.loop(0, 7)
    def _(buf):
        @pl.when(buf == SIB)
        def _():
            arrived(SIB, 0, 1, EDGE, OUTER, 2, 3)
            relay(RELAY, EDGE)
            arrived(SIDE, 0, 1, EDGE, 2, 3)
            send(OUTER, RELAY)

        @pl.when(buf == SIDE)
        def _():
            arrived(SIDE, OUTER)
            arrived(SIB_ACROSS, 0, 1, EDGE, OUTER, 2, 3)

        @pl.when(buf == ACROSS)
        def _():
            relay(RELAY, 2)

        @pl.when(buf == SIB_ACROSS)
        def _():
            relay(RELAY, OUTER)
            relay(RELAY, 3)

        @pl.when(buf == SIB_RELAY)
        def _():
            arrived(SIB_RELAY, 0, 1, EDGE, OUTER, 2, 3)

        contribute(buf)

    for buf in range(7):
        for part in range(7):
            if buf != OWN or part == OUTER:
                copy(buf, part).wait_send()


def per_device(history, panel_pos, area, observer_pos, delays):
    vmem = pl.BlockSpec(memory_space=pltpu.VMEM)
    return pl.pallas_call(
        kernel,
        out_shape=jax.ShapeDtypeStruct((1024, 256), jnp.float32),
        in_specs=[vmem, vmem, vmem, vmem, pl.BlockSpec(memory_space=pltpu.SMEM)],
        out_specs=vmem,
        scratch_shapes=[
            pltpu.VMEM((7, 4, EXT, 256), jnp.bfloat16),
            pltpu.VMEM((7, 8, 256), jnp.float32),
            pltpu.VMEM((7, 1024, COEF * 256), jnp.bfloat16),
            pltpu.VMEM((COEF * 256, 256), jnp.bfloat16),
            pltpu.VMEM((2, STAGE, 128), jnp.float32),
            pltpu.VMEM((3, 1024, 128), jnp.float32),
            pltpu.SMEM((8,), jnp.int32),
            pltpu.SemaphoreType.DMA((7, 7)),
            pltpu.SemaphoreType.DMA((7, 7)),
        ],
        compiler_params=pltpu.CompilerParams(
            collective_id=0, has_side_effects=True, vmem_limit_bytes=56 * 1024 * 1024),
        cost_estimate=pl.CostEstimate(flops=6_580_000_000, bytes_accessed=2_000_000, transcendentals=1_900_000),
    )(history, panel_pos, area, observer_pos, delays)


def solution(mesh):
    return jax.shard_map(
        per_device,
        mesh=mesh,
        in_specs=(P(None, "blk", "tm"), P(None, "blk"), P("blk"), P(None, "blk"), P("blk", None)),
        out_specs=P("blk", "tm"),
        check_vma=False,
    )
```

```python
import math

import jax
import jax.numpy as jnp
from jax import lax
from jax.experimental import pallas as pl
from jax.experimental.pallas import tpu as pltpu
from jax.sharding import PartitionSpec as P

MESH = pl.DeviceIdType.MESH
MAIN, HALO = 256, 80
BODY = MAIN - HALO
EXT = MAIN + HALO
STAGE = HALO + MAIN + HALO
COEF = 7
INV_FOUR_PI = 1.0 / (4.0 * math.pi)
OWN, SIB, ACROSS, SIDE, SIB_ACROSS, RELAY, SIB_RELAY = range(7)
EDGE, OUTER, GEOM = 4, 5, 6


def kernel(history, place, area, observers, delays, out,
           ext, geom, weights, signals, stage, spread, lags, send_sem, recv_sem):
    g = lax.axis_index("blk")
    half = lax.axis_index("tm")
    blocks = lax.axis_size("blk")
    core = g % 2
    upper = (g // 2) % 2
    sign = 1 - 2 * upper
    inner = (core + upper) % 2
    sibling = g + 1 - 2 * core
    across = g + 2 * sign
    ahead = (g + 4 * sign + blocks) % blocks
    behind = (g - 4 * sign + blocks) % blocks
    beside = (sibling + 4 * sign * (2 * inner - 1) + blocks) % blocks
    facing = g + inner * sign
    target = {SIB: sibling, ACROSS: across, SIDE: beside, SIB_ACROSS: sibling, RELAY: ahead, SIB_RELAY: sibling}
    origin = {SIB: OWN, ACROSS: OWN, SIDE: OWN, SIB_ACROSS: ACROSS, RELAY: ACROSS, SIB_RELAY: RELAY}
    slot = {OWN: 3, SIB: 4 - 2 * inner, ACROSS: 5, SIDE: 6 * inner, SIB_ACROSS: 6 - 2 * inner, RELAY: 1,
            SIB_RELAY: 2 - 2 * inner}
    edge_rows = pl.ds(pl.multiple_of(BODY * (1 - half), 16), HALO)
    body_rows = pl.ds(pl.multiple_of(HALO * half, 16), BODY)
    outer_rows = pl.ds(MAIN, HALO)

    barrier = pltpu.get_barrier_semaphore()
    for device, part in ((sibling, half), (across, half), (ahead, half), (behind, half), (beside, half),
                         (g, 1 - half), (across, 1 - half), (facing, 1 - half)):
        pl.semaphore_signal(barrier, inc=1, device_id=(device, part), device_id_type=MESH)

    geom[OWN] = jnp.zeros((8, 256), jnp.float32)
    geom[OWN, 0:3, :] = place[...].astype(jnp.float32)
    geom[OWN, 3:4, :] = area[...].astype(jnp.float32).reshape(1, 256) * INV_FOUR_PI
    for buf, m in slot.items():
        lags[buf] = delays[0, m + upper * (6 - 2 * m)]

    def flip(c):
        ext[OWN, c, 0:MAIN, :] = history[c].T

    def view(buf, part):
        if part == GEOM:
            return geom.at[buf]
        if part == EDGE:
            return ext.at[buf, :, edge_rows]
        if part == OUTER:
            return ext.at[buf, :, outer_rows]
        return ext.at[buf, part, body_rows]

    def copy(buf, part):
        if part == OUTER and buf in (OWN, ACROSS, RELAY):
            source = {OWN: OWN, ACROSS: OWN, RELAY: RELAY - (RELAY - SIDE) * inner}[buf]
            device = {OWN: g, ACROSS: across, RELAY: facing}[buf]
            src, where = view(source, EDGE), (device, 1 - half)
        else:
            src, where = view(origin[buf], part), (target[buf], half)
        return pltpu.make_async_remote_copy(
            src_ref=src, dst_ref=view(buf, part), send_sem=send_sem.at[buf, part], recv_sem=recv_sem.at[buf, part],
            device_id=where, device_id_type=MESH)

    def fill_weights(buf):
        @pl.loop(0, 16, unroll=4)
        def _(i):
            rows = pl.ds(pl.multiple_of(i * 64, 64), 64)
            ox, oy, oz = (spread[n, rows, :] for n in range(3))
            for lane in (0, 128):
                cols = pl.ds(lane, 128)
                dx = ox - geom[buf, 0:1, cols]
                dy = oy - geom[buf, 1:2, cols]
                dz = oz - geom[buf, 2:3, cols]
                inv = lax.rsqrt(dx * dx + dy * dy + dz * dz)
                s = geom[buf, 3:4, cols] * inv
                fast = s * inv
                fx, fy, fz = fast * dx, fast * dy, fast * dz
                for n, value in enumerate((s, fx, fx * inv, fy, fy * inv, fz, fz * inv)):
                    weights[buf, rows, pl.ds(n * 256 + lane, 128)] = value.astype(jnp.bfloat16)

    def fill_signals(buf, c):
        k = lags[buf]
        edge = ext[buf, c, MAIN:EXT, :].astype(jnp.float32)
        zero = jnp.zeros_like(edge)
        late = half == 1
        for lane in (0, 1):
            cols = slice(lane * 128, lane * 128 + 128)
            stage[lane, 0:HALO, :] = jnp.where(late, edge, zero)[:, cols]
            stage[lane, HALO:HALO + MAIN, :] = ext[buf, c, 0:MAIN, cols].astype(jnp.float32)
            stage[lane, HALO + MAIN:STAGE, :] = jnp.where(late, zero, edge)[:, cols]
            after = stage[lane, pl.ds(HALO + 1 - k, MAIN), :]
            before = stage[lane, pl.ds(HALO - 1 - k, MAIN), :]
            at = max(2 * c - 1, 0) * 256 + lane * 128
            signals[at:at + 128, :] = (0.5 * (after - before)).astype(jnp.bfloat16).T
            if c:
                signals[at + 256:at + 384, :] = stage[lane, pl.ds(HALO - k, MAIN), :].astype(jnp.bfloat16).T

    def contribute(buf, channels=(0, 1, 2, 3), first=False):
        for c in channels:
            fill_signals(buf, c)
        cols = slice(max(2 * channels[0] - 1, 0) * 256, (2 * channels[-1] + 1) * 256)
        part = jnp.dot(weights[buf, :, cols], signals[cols, :], preferred_element_type=jnp.float32)
        if first:
            out[...] = part
        else:
            out[...] += part

    def arrived(buf, *parts):
        for part in parts:
            copy(buf, part).wait_recv()

    def send(part, *bufs):
        for buf in bufs:
            copy(buf, part).start()

    def relay(buf, part):
        arrived(buf, part)
        if buf == RELAY:
            send(part, SIB_RELAY)
        elif part == OUTER:
            send(part, SIB_ACROSS)
        else:
            send(part, RELAY, SIB_ACROSS)

    flip(0)
    pl.semaphore_wait(barrier, 8)
    send(GEOM, ACROSS, SIDE, SIB)
    send(0, ACROSS, SIDE, SIB)
    flip(1)
    send(1, ACROSS, SIDE, SIB)
    flip(2)
    flip(3)
    send(EDGE, ACROSS, SIDE)
    send(OUTER, OWN, ACROSS)
    send(2, ACROSS, SIDE)
    send(3, ACROSS, SIDE)
    send(EDGE, SIB)
    send(2, SIB)
    send(3, SIB)
    for axis in range(3):
        for i in range(8):
            line = observers[axis:axis + 1, i * 128:(i + 1) * 128]
            spread[axis, i * 128:(i + 1) * 128, :] = jnp.broadcast_to(line, (128, 128)).T

    fill_weights(OWN)
    relay(ACROSS, GEOM)
    arrived(SIB, GEOM)
    fill_weights(SIB)
    relay(ACROSS, 0)
    arrived(SIDE, GEOM)
    fill_weights(SIDE)
    relay(ACROSS, 1)
    fill_weights(ACROSS)
    arrived(SIB_ACROSS, GEOM)
    fill_weights(SIB_ACROSS)
    relay(ACROSS, EDGE)
    relay(RELAY, GEOM)
    arrived(OWN, OUTER)
    send(OUTER, SIDE, SIB)
    fill_weights(RELAY)
    relay(RELAY, 0)
    relay(ACROSS, OUTER)
    relay(ACROSS, 2)
    arrived(SIB_RELAY, GEOM)
    fill_weights(SIB_RELAY)
    relay(RELAY, 1)
    relay(ACROSS, 3)
    out[...] = jnp.zeros_like(out)

    @pl.loop(0, 7)
    def _(buf):
        @pl.when(buf == SIB)
        def _():
            arrived(SIB, 0, 1, EDGE, OUTER, 2, 3)
            relay(RELAY, EDGE)
            arrived(SIDE, 0, 1, EDGE, 2, 3)
            send(OUTER, RELAY)

        @pl.when(buf == SIDE)
        def _():
            arrived(SIDE, OUTER)
            arrived(SIB_ACROSS, 0, 1, EDGE, OUTER, 2, 3)

        @pl.when(buf == ACROSS)
        def _():
            relay(RELAY, 2)

        @pl.when(buf == SIB_ACROSS)
        def _():
            relay(RELAY, OUTER)

        @pl.when(buf == RELAY)
        def _():
            relay(RELAY, 3)

        @pl.when(buf == SIB_RELAY)
        def _():
            arrived(SIB_RELAY, 0, 1, EDGE, OUTER, 2, 3)

        contribute(buf)

    for buf in range(7):
        for part in range(7):
            if buf != OWN or part == OUTER:
                copy(buf, part).wait_send()


def per_device(history, panel_pos, area, observer_pos, delays):
    vmem = pl.BlockSpec(memory_space=pltpu.VMEM)
    return pl.pallas_call(
        kernel,
        out_shape=jax.ShapeDtypeStruct((1024, 256), jnp.float32),
        in_specs=[vmem, vmem, vmem, vmem, pl.BlockSpec(memory_space=pltpu.SMEM)],
        out_specs=vmem,
        scratch_shapes=[
            pltpu.VMEM((7, 4, EXT, 256), jnp.bfloat16),
            pltpu.VMEM((7, 8, 256), jnp.float32),
            pltpu.VMEM((7, 1024, COEF * 256), jnp.bfloat16),
            pltpu.VMEM((COEF * 256, 256), jnp.bfloat16),
            pltpu.VMEM((2, STAGE, 128), jnp.float32),
            pltpu.VMEM((3, 1024, 128), jnp.float32),
            pltpu.SMEM((8,), jnp.int32),
            pltpu.SemaphoreType.DMA((7, 7)),
            pltpu.SemaphoreType.DMA((7, 7)),
        ],
        compiler_params=pltpu.CompilerParams(
            collective_id=0, has_side_effects=True, vmem_limit_bytes=56 * 1024 * 1024),
        cost_estimate=pl.CostEstimate(flops=6_580_000_000, bytes_accessed=2_000_000, transcendentals=1_900_000),
    )(history, panel_pos, area, observer_pos, delays)


def solution(mesh):
    return jax.shard_map(
        per_device,
        mesh=mesh,
        in_specs=(P(None, "blk", "tm"), P(None, "blk"), P("blk"), P(None, "blk"), P("blk", None)),
        out_specs=P("blk", "tm"),
        check_vma=False,
    )
```
